128 devices in a mesh: dp: 64 (over x_hi, y, z, core), mp: 2 (over x_lo).
Axes of the slice: x: 4 (x_hi: 2, x_lo: 2; x = x_hi * 2 + x_lo), y: 4, z: 4, core: 2. Of those that a mesh axis runs over, the one named last changes fastest.
Arguments:
- image_emb: bfloat16 [8192, 1152], P('dp', 'mp'), may hold values from -0.1875 to 0.1875
- caption_emb: bfloat16 [12288, 1152], P('dp', 'mp'), may hold values from -0.1875 to 0.1875
- caption_count: int32 [8192], P('dp'), may hold values from 1 to 5, as said below
- caption_owner: int32 [12288], P('dp'), may hold values from 0 to 63, as said below
- pair_image: int32 [16384], P('dp'), may hold values from -1 to 127, as said below
Outputs:
- image_grad: bfloat16 [8192, 1152], P('dp', 'mp')
- caption_grad: bfloat16 [12288, 1152], P('dp', 'mp')
The draws below stay inside these ranges and needn't reach their ends.
Inputs may be any that keep to these rules, and one draw needn't show every extreme that they name: `caption_owner`: each loader sends either 2 or 4 of its rows to each owner; some owner receives 4 rows from every loader. `pair_image`: slot s * 4 + r of owner o names an image exactly when loader s sends more than r rows to o, and holds -1 otherwise; every image of the owner is named at least once. caption_count[i] is the number of slots that name image i.
All inputs are finite; a program needn't handle non-finite values.
Results may differ from the reference program's by a relative error of at most 0.0013.
The reference program's roundings to bfloat16 on the way (of `coefficient`) count: a program that leaves them out, or rounds other values in their place, can miss the bound.
Values may be sent and summed in bfloat16 or wider, within the bound.
No kernel may reach another device: no remote copies, remote signals or barrier semaphores. Data moves between devices by JAX's collectives and lax.ppermute only.
A program may use at most 192 MiB of HBM per device.

```python
import jax
import jax.numpy as jnp
from jax import lax

D = 1152
CAP_DEV = 256
IMG_DEV = 128
LOAD_DEV = 192
IMAGES = 8192
CAPTIONS = 12288
N_DP = 64


def layout_tables(key):
    groups = N_DP
    per_owner = CAP_DEV // groups
    half_slots = per_owner // 2
    images_dev = CAP_DEV // 2
    quarter = images_dev // 4
    keys = jax.random.split(key, 6)
    owner_order = jax.random.permutation(keys[0], groups)
    pair_sizes = jax.random.randint(keys[1], (groups // 2,), 0, groups + 1)
    pair_sizes = pair_sizes.at[0].set(groups)
    offsets = jax.random.randint(keys[2], (groups // 2,), 0, groups)
    sources = jnp.arange(groups, dtype=jnp.int32)
    inside = jnp.mod(sources[:, None] - offsets[None, :], groups) < pair_sizes[None, :]
    by_rank = jnp.stack([inside, jnp.logical_not(inside)], axis=2).reshape(groups, groups)
    position = jnp.argsort(owner_order)
    full_rows = by_rank[:, position]
    sent = half_slots + half_slots * full_rows.astype(jnp.int32)
    slot_ids = jnp.arange(CAP_DEV, dtype=jnp.int32)
    loader_live = jnp.mod(slot_ids, per_owner)[None, :] < sent[:, slot_ids // per_owner]
    scores = jax.random.randint(keys[3], (groups, CAP_DEV), 0, 2 ** 19) * CAP_DEV + slot_ids[None, :]
    scores = jnp.where(loader_live, scores, 2 ** 30 + slot_ids[None, :])
    loader_slots = jnp.argsort(scores, axis=1)[:, :LOAD_DEV]
    caption_owner = (loader_slots // per_owner).reshape(-1).astype(jnp.int32)
    owner_live = jnp.mod(slot_ids, per_owner)[None, :] < jnp.transpose(sent)[:, slot_ids // per_owner]
    owner_load = jnp.sum(owner_live.astype(jnp.int32), axis=1)
    live_rank = jnp.maximum(jnp.cumsum(owner_live.astype(jnp.int32), axis=1) - 1, 0)
    token_scores = jax.random.randint(keys[4], (groups, CAP_DEV), 0, 2 ** 19) * CAP_DEV + slot_ids[None, :]
    token_scores = jnp.where(slot_ids[None, :] < owner_load[:, None], token_scores, 2 ** 30 + slot_ids[None, :])
    token_order = jnp.argsort(token_scores, axis=1)
    image_ids = jnp.arange(images_dev, dtype=jnp.int32)
    image_scores = jax.random.randint(keys[5], (groups, images_dev), 0, 2 ** 19) * images_dev + image_ids[None, :]
    extra_order = jnp.argsort(image_scores, axis=1)
    token = jnp.take_along_axis(token_order, live_rank, axis=1)
    extra_image = jnp.take_along_axis(extra_order, jnp.mod(jnp.maximum(token - images_dev, 0), quarter), axis=1)
    token_image = jnp.where(token < images_dev, token, extra_image)
    pair_image = jnp.where(owner_live, token_image, -1).reshape(-1).astype(jnp.int32)
    extras = owner_load - images_dev
    extra_target = jnp.take_along_axis(extra_order, jnp.broadcast_to(jnp.mod(image_ids, quarter)[None, :], (groups, images_dev)), axis=1)
    active = image_ids[None, :] < extras[:, None]
    hits = (extra_target[:, :, None] == image_ids[None, None, :]) & active[:, :, None]
    caption_count = (1 + jnp.sum(hits.astype(jnp.int32), axis=1)).reshape(-1).astype(jnp.int32)
    return (caption_count, caption_owner, pair_image)


def draw_caption_count(key, part):
    tables = layout_tables(key)
    return tables[0]


def draw_caption_owner(key, part):
    tables = layout_tables(key)
    return tables[1]


def draw_pair_image(key, part):
    tables = layout_tables(key)
    return tables[2]


def block_levels(stream_key, shape, shards, least, high):
    factor_of = 1.0
    for axis_at, parts in shards:
        steps = jax.random.uniform(jax.random.fold_in(jax.random.fold_in(stream_key, 6), axis_at), (parts,), jnp.float32, least / len(shards), high / len(shards))
        factor_of = factor_of * jnp.repeat(jnp.exp(steps), shape[axis_at] // parts).reshape((-1,) + (1,) * (len(shape) - 1 - axis_at))
    return factor_of


def scatter_about(rng, extent, width, reach, cuts=(), kind=jnp.bfloat16):
    level = block_levels(rng, extent, cuts, -0.22, 0.18) if cuts else 1.0
    array = jax.random.normal(rng, extent, jnp.float32) * width * level
    return jnp.minimum(jnp.maximum(array, -reach), reach).astype(kind)


def setup_inputs(seed: int = 0) -> dict:
    streams_of = jax.random.split(jax.random.key(seed), 6)
    return {
        "image_emb": scatter_about(streams_of[0], (IMAGES, D), (D ** -0.5), 0.1875, ((0, 64), (1, 2))),
        "caption_emb": scatter_about(streams_of[1], (CAPTIONS, D), (D ** -0.5), 0.1875, ((0, 64), (1, 2))),
        "caption_count": draw_caption_count(jax.random.fold_in(streams_of[5], 71), 0),
        "caption_owner": draw_caption_owner(jax.random.fold_in(streams_of[5], 71), 0),
        "pair_image": draw_pair_image(jax.random.fold_in(streams_of[5], 71), 0),
    }


logit_scale = 10.0
logit_bias = -2.0


def caption_images(caption_owner, pair_image):
    per_owner = CAP_DEV // N_DP
    owners = caption_owner.reshape(N_DP, LOAD_DEV)
    positions = jnp.arange(LOAD_DEV, dtype=jnp.int32)
    earlier = positions[None, :] < positions[:, None]

    def ranks(row):
        same_owner = row[:, None] == row[None, :]
        return jnp.sum((same_owner & earlier).astype(jnp.int32), axis=1).astype(jnp.int32)

    rank_index = lax.map(ranks, owners)
    source = jnp.arange(N_DP, dtype=jnp.int32)[:, None]
    slot_index = (owners * CAP_DEV + source * per_owner + rank_index).astype(jnp.int32)
    local_image = jnp.take(pair_image, slot_index.reshape(-1))
    return (caption_owner * IMG_DEV + local_image).astype(jnp.int32)


def reference(image_emb, caption_emb, caption_count, caption_owner, pair_image):
    image_of = caption_images(caption_owner, pair_image).reshape(N_DP, LOAD_DEV)
    blocks = caption_emb.reshape(N_DP, LOAD_DEV, D)
    inverse_count = 1.0 / caption_count.astype(jnp.float32)
    image_rows = jnp.arange(IMAGES, dtype=jnp.int32)

    def visit_block(total, item):
        block_rows, block_images = item
        products = lax.dot_general(image_emb, block_rows, (((1,), (1,)), ((), ())), preferred_element_type=jnp.float32)
        logits = logit_scale * products + logit_bias
        positive = (block_images[None, :] == image_rows[:, None]).astype(jnp.float32)
        weight = 1.0 + positive * (inverse_count[:, None] - 1.0)
        coefficient = (logit_scale * weight * (jax.nn.sigmoid(logits) - positive)).astype(jnp.bfloat16)
        total = total + jnp.dot(coefficient, block_rows, preferred_element_type=jnp.float32)
        block_grad = lax.dot_general(coefficient, image_emb, (((0,), (0,)), ((), ())), preferred_element_type=jnp.float32)
        return total, block_grad.astype(jnp.bfloat16)

    total, grads = lax.scan(visit_block, jnp.zeros((IMAGES, D), jnp.float32), (blocks, image_of))
    return total.astype(jnp.bfloat16), grads.reshape(CAPTIONS, D)
```

```python
import jax
import jax.numpy as jnp
from jax import lax
from jax.experimental import pallas as pl
from jax.experimental.pallas import tpu as pltpu
from jax.sharding import PartitionSpec as P


F = 576
W = 640
IMG = 128
ROWS = F + 16
HALF = 96
CAPS = 8 * HALF
IMGS = 8 * IMG
VMEM_LIMIT = 56 * 1024 * 1024


def exchange(value, move):
    pairs = []
    for source in range(128):
        xl, c, z, y, xh = source & 1, source >> 1 & 1, source >> 2 & 3, source >> 4 & 3, source >> 6
        jx, jy, jz, jc = move(c)
        x = (xh * 2 + xl) ^ jx
        target = ((((x >> 1) * 4 + (y ^ jy)) * 4 + (z ^ jz)) * 2 + (c ^ jc)) * 2 + (x & 1)
        pairs.append((source, target))
    return lax.ppermute(value, ("dp", "mp"), pairs)


def first_axis(j):
    return lambda c: (j, 0, 0, 0) if c == 0 else (0, j, 0, 0)


def second_axis(j):
    return lambda c: (0, j, 0, 0) if c == 0 else (j, 0, 0, 0)


def caption_kernel(near_ref, far_ref, rows_ref, turned_ref):
    for e, ref in enumerate((near_ref, far_ref)):
        for j in range(4):
            for h in range(2):
                rows_ref[pl.ds((e * 4 + j) * HALF, HALF), h * W : (h + 1) * W] = ref[j, h]
    for block in range(2 * W // 128):
        columns = slice(block * 128, (block + 1) * 128)
        turned_ref[columns, :] = rows_ref[:, columns].T


def main_kernel(
    place_ref, captions_ref, turned_ref, p0_ref, p1_ref, p2_ref, p3_ref,
    image_out, caption_out, images, tables, coefficient, sems,
):
    me = place_ref[0]
    c = me & 1
    copies = []
    for p2, ref in enumerate((p0_ref, p1_ref, p2_ref, p3_ref)):
        for p1 in range(4):
            jx = jnp.where(c == 0, p1, p2)
            jy = jnp.where(c == 0, p2, p1)
            h, column = jx & 1, jy * 2 + (jx >> 1)
            copies.append(
                pltpu.make_async_copy(
                    ref.at[p1, pl.ds(0, F)],
                    images.at[h, pl.ds(0, F), pl.ds(pl.multiple_of(column * IMG, IMG), IMG)],
                    sems.at[0, p2 * 4 + p1],
                )
            )
            copies.append(
                pltpu.make_async_copy(
                    ref.at[p1, pl.ds(F, 16)], tables.at[h, column], sems.at[1, p2 * 4 + p1]
                )
            )
    for copy in copies:
        copy.start()
    images[:, F:W, :] = jnp.zeros((2, W - F, IMGS), jnp.bfloat16)
    marks = captions_ref[:, 512:640].astype(jnp.float32).astype(jnp.int32)
    owner, slot = marks[:, 64:65], marks[:, 65:66]
    relative = owner ^ me
    for copy in copies:
        copy.wait()

    table = tables[0].astype(jnp.float32)
    inverse = 1.0 / table[:, 0, :]
    slots = jnp.concatenate([table[:, 1, :], table[:, 2, :]], axis=1)
    slots = jnp.concatenate([slots, jnp.zeros((120, 256), jnp.float32)], axis=0)
    picked = (lax.broadcasted_iota(jnp.int32, (CAPS, 256), 1) == slot).astype(jnp.float32)
    named = lax.dot_general(
        picked.astype(jnp.bfloat16), slots.astype(jnp.bfloat16), (((1,), (1,)), ((), ())),
        preferred_element_type=jnp.float32,
    )
    block = (relative >> 3 & 3) * 2 + (relative >> 5)
    lanes = lax.broadcasted_iota(jnp.int32, (CAPS, 128), 1)
    named = jnp.sum(jnp.where(lanes == block, named, 0.0), axis=1, keepdims=True)
    target = jnp.where((relative & 7) == 0, block * IMG + named.astype(jnp.int32), -1)

    for jy in range(4):
        columns = slice(jy * 256, (jy + 1) * 256)
        products = jnp.dot(
            captions_ref[:, :W], images[0, :, columns], preferred_element_type=jnp.float32
        ) + jnp.dot(captions_ref[:, W:], images[1, :, columns], preferred_element_type=jnp.float32)
        negative = 5.0 * jnp.tanh(5.0 * products - 1.0) + 5.0
        weight = jnp.concatenate([inverse[2 * jy : 2 * jy + 1], inverse[2 * jy + 1 : 2 * jy + 2]], axis=1)
        here = lax.broadcasted_iota(jnp.int32, (CAPS, 256), 1) + jy * 256 == target
        part = jnp.where(here, weight * (negative - 10.0), negative).astype(jnp.bfloat16)
        coefficient[:, columns] = part
        for h in range(2):
            grads = jnp.dot(
                turned_ref[h * W : h * W + F, :], part, preferred_element_type=jnp.float32
            )
            for g in range(2):
                jx = g * 2 + h
                p2 = jnp.where(c == 0, jy, jx)
                p1 = jnp.where(c == 0, jx, jy)
                image_out[p2, p1] = grads[:, g * IMG : (g + 1) * IMG]
    for h in range(2):
        for start, size in ((0, 256), (256, 256), (512, 128)):
            caption_out[:, h * W + start : h * W + start + size] = lax.dot_general(
                coefficient[...], images[h, start : start + size, :], (((1,), (1,)), ((), ())),
                preferred_element_type=jnp.float32,
            )


def body(image_emb, caption_emb, caption_count, caption_owner, pair_image):
    me = lax.axis_index("dp")
    xl = lax.axis_index("mp")

    positions = jnp.arange(192, dtype=jnp.int32)
    earlier = positions[None, :] < positions[:, None]
    same_owner = caption_owner[:, None] == caption_owner[None, :]
    rank = jnp.sum((same_owner & earlier).astype(jnp.int32), axis=1)
    slot = me * 4 + rank
    marks = jnp.stack([caption_owner, slot], axis=1).astype(jnp.bfloat16)
    rows = jnp.concatenate([caption_emb, marks, jnp.zeros((192, W - F - 2), jnp.bfloat16)], axis=1)
    kept = lax.dynamic_slice_in_dim(rows, xl * HALF, HALF, 0)
    given = lax.dynamic_slice_in_dim(rows, (1 - xl) * HALF, HALF, 0)

    extra = jnp.concatenate(
        [caption_count[None], pair_image.reshape(2, IMG), jnp.zeros((13, IMG), jnp.int32)], axis=0
    ).astype(jnp.bfloat16)
    piece = jnp.concatenate([image_emb.T, extra], axis=0)

    pieces = [piece] + [exchange(piece, first_axis(j)) for j in (1, 2, 3)]
    gained = exchange(given, lambda c: (1, 0, 0, 0))
    pieces = jnp.stack(pieces)
    groups = [pieces] + [exchange(pieces, second_axis(j)) for j in (1, 2, 3)]

    pair = jnp.stack([kept, gained])
    near = jnp.stack([pair] + [exchange(pair, lambda c, j=j: (0, 0, j, 0)) for j in (1, 2, 3)])
    far = exchange(near, lambda c: (0, 0, 0, 1))

    vmem = pl.BlockSpec(memory_space=pltpu.VMEM)
    anywhere = pl.BlockSpec(memory_space=pl.ANY)
    captions, turned = pl.pallas_call(
        caption_kernel,
        out_shape=(
            jax.ShapeDtypeStruct((CAPS, 2 * W), jnp.bfloat16),
            jax.ShapeDtypeStruct((2 * W, CAPS), jnp.bfloat16),
        ),
        in_specs=[vmem] * 2,
        out_specs=(vmem, vmem),
        compiler_params=pltpu.CompilerParams(vmem_limit_bytes=VMEM_LIMIT),
        cost_estimate=pl.CostEstimate(flops=0, bytes_accessed=8_000_000, transcendentals=0),
    )(near, far)

    image_part, caption_part = pl.pallas_call(
        main_kernel,
        out_shape=(
            jax.ShapeDtypeStruct((4, 4, F, IMG), jnp.float32),
            jax.ShapeDtypeStruct((CAPS, 2 * W), jnp.float32),
        ),
        in_specs=[pl.BlockSpec(memory_space=pltpu.SMEM), vmem, vmem] + [anywhere] * 4,
        out_specs=(vmem, vmem),
        scratch_shapes=[
            pltpu.VMEM((2, W, IMGS), jnp.bfloat16),
            pltpu.VMEM((2, 8, 16, IMG), jnp.bfloat16),
            pltpu.VMEM((CAPS, IMGS), jnp.bfloat16),
            pltpu.SemaphoreType.DMA((2, 16)),
        ],
        compiler_params=pltpu.CompilerParams(vmem_limit_bytes=VMEM_LIMIT),
        cost_estimate=pl.CostEstimate(
            flops=6 * CAPS * IMGS * 2 * W, bytes_accessed=16_000_000, transcendentals=CAPS * IMGS
        ),
    )(me[None], captions, turned, *groups)

    half = jnp.float16
    caption_part = caption_part.reshape(2, 4, HALF, 2 * W)
    crossed = exchange(caption_part[1].astype(half), lambda c: (0, 0, 0, 1))
    group_total = caption_part[0] + crossed.astype(jnp.float32)
    image_received = [
        exchange(image_part[j].astype(half), second_axis(j)) for j in (2, 1, 3)
    ]
    caption_received = [
        exchange(group_total[j].astype(half), lambda c, j=j: (0, 0, j, 0)) for j in (2, 1, 3)
    ]
    line = image_part[0]
    for value in image_received:
        line = line + value.astype(jnp.float32)
    line_received = [exchange(line[j].astype(half), first_axis(j)) for j in (2, 1, 3)]
    total = line[0]
    for value in line_received:
        total = total + value.astype(jnp.float32)
    image_grad = total.astype(jnp.bfloat16).T

    both = group_total[0]
    for value in caption_received:
        both = both + value.astype(jnp.float32)
    both = both.astype(jnp.bfloat16)
    mine, theirs = both[:, :F], both[:, W : W + F]
    returned = exchange(theirs, lambda c: (1, 0, 0, 0))
    caption_grad = jnp.where(
        xl == 0,
        jnp.concatenate([mine, returned], axis=0),
        jnp.concatenate([returned, mine], axis=0),
    )
    return image_grad, caption_grad


def solution(mesh):
    in_specs = (P("dp", "mp"), P("dp", "mp"), P("dp"), P("dp"), P("dp"))
    out_specs = (P("dp", "mp"), P("dp", "mp"))
    return jax.shard_map(body, mesh=mesh, in_specs=in_specs, out_specs=out_specs, check_vma=False)
```

```python
import functools

import jax
import jax.numpy as jnp
from jax import lax
from jax.experimental import pallas as pl
from jax.experimental.pallas import tpu as pltpu
from jax.sharding import PartitionSpec as P


F = 576
W = 640
IMG = 128
ROWS = F + 16
LOAD = 192
HALF = 96
CAPS = 8 * HALF
COLS = 4 * IMG


def exchange(value, move):
    pairs = []
    for source in range(128):
        xl, c, z, y, xh = source & 1, source >> 1 & 1, source >> 2 & 3, source >> 4 & 3, source >> 6
        jx, jy, jz, jc = move(c)
        x = (xh * 2 + xl) ^ jx
        target = ((((x >> 1) * 4 + (y ^ jy)) * 4 + (z ^ jz)) * 2 + (c ^ jc)) * 2 + (x & 1)
        pairs.append((source, target))
    return lax.ppermute(value, ("dp", "mp"), pairs)


def first_axis(j):
    return lambda c: (j, 0, 0, 0) if c == 0 else (0, j, 0, 0)


def second_axis(j):
    return lambda c: (0, j, 0, 0) if c == 0 else (j, 0, 0, 0)


def along_z(j):
    return lambda c: (0, 0, j, 0)


def other_half(c):
    return (1, 0, 0, 0)


def other_core(c):
    return (0, 0, 0, 1)


def join_kernel(piece_ref, r1_ref, r2_ref, r3_ref, kept_ref, gained_ref, pieces_ref, pair_ref):
    for i, ref in enumerate((piece_ref, r1_ref, r2_ref, r3_ref)):
        pieces_ref[i] = ref[...]
    pair_ref[0] = kept_ref[...]
    pair_ref[1] = gained_ref[...]


def near_kernel(pair_ref, r1_ref, r2_ref, r3_ref, _a, _b, near_ref):
    for i, ref in enumerate((pair_ref, r1_ref, r2_ref, r3_ref)):
        near_ref[i] = ref[...]


def load_images(c, refs, images, tables, sems):
    copies = []
    for low, ref in enumerate(refs):
        for p1 in range(4):
            h = jnp.where(c == 0, p1 & 1, low)
            q = jnp.where(c == 0, low * 2 + (p1 >> 1), p1)
            copies.append(
                pltpu.make_async_copy(
                    ref.at[p1, pl.ds(0, F)],
                    images.at[pl.ds(pl.multiple_of(h * W, W), F), pl.ds(pl.multiple_of(q * IMG, IMG), IMG)],
                    sems.at[0, low * 4 + p1],
                )
            )
            copies.append(
                pltpu.make_async_copy(
                    ref.at[p1, pl.ds(F, 16)], tables.at[h, q], sems.at[1, low * 4 + p1]
                )
            )
    for copy in copies:
        copy.start()
    return copies


def make_coefficients(stage, me, captions_ref, images, tables, coefficient, copies):
    c = me & 1
    for h in range(2):
        images[h * W + F : (h + 1) * W, :] = jnp.zeros((W - F, COLS), jnp.bfloat16)
    marks = captions_ref[:, 512:640].astype(jnp.float32).astype(jnp.int32)
    owner, slot = marks[:, 64:65], marks[:, 65:66]
    relative = owner ^ me
    near_y, near_x = relative >> 3 & 3, relative >> 5
    column = jnp.where(c == 0, near_y * 2 + near_x, near_x * 4 + near_y) - 4 * stage
    picked = (lax.broadcasted_iota(jnp.int32, (CAPS, 256), 1) == slot).astype(jnp.float32)
    for copy in copies:
        copy.wait()

    table = tables[0].astype(jnp.float32)
    inverse = 1.0 / table[:, 0, :]
    slots = jnp.concatenate([table[:, 1, :], table[:, 2, :]], axis=1)
    slots = jnp.concatenate([slots, jnp.zeros((124, 256), jnp.float32)], axis=0)
    named = lax.dot_general(
        picked.astype(jnp.bfloat16), slots.astype(jnp.bfloat16), (((1,), (1,)), ((), ())),
        preferred_element_type=jnp.float32,
    )
    lanes = lax.broadcasted_iota(jnp.int32, (CAPS, 128), 1)
    named = jnp.sum(jnp.where(lanes == column, named, 0.0), axis=1, keepdims=True)
    inside = ((relative & 7) == 0) & (column >= 0) & (column < 4)
    target = jnp.where(inside, column * IMG + named.astype(jnp.int32), -1)

    for u in range(2):
        columns = slice(u * 256, (u + 1) * 256)
        products = jnp.dot(
            captions_ref[...], images[:, columns], preferred_element_type=jnp.float32
        )
        negative = 5.0 * jnp.tanh(5.0 * products - 1.0) + 5.0
        weight = jnp.concatenate([inverse[2 * u : 2 * u + 1], inverse[2 * u + 1 : 2 * u + 2]], axis=1)
        here = lax.broadcasted_iota(jnp.int32, (CAPS, 256), 1) + u * 256 == target
        part = jnp.where(here, weight * (negative - 10.0), negative)
        coefficient[:, columns] = part.astype(jnp.bfloat16)


def image_grads(c, turned_ref, coefficient, a_out, b_out):
    for low, out in enumerate((a_out, b_out)):
        for t in range(2):
            u = jnp.where(c == 0, low, t)
            h = jnp.where(c == 0, t, low)
            grads = jnp.dot(
                turned_ref[pl.ds(pl.multiple_of(h * W, W), F), :],
                coefficient[:, pl.ds(pl.multiple_of(u * 256, 256), 256)],
                preferred_element_type=jnp.float32,
            )
            for g in range(2):
                p1 = jnp.where(c == 0, g * 2 + t, t * 2 + g)
                out[p1] = grads[:, g * IMG : (g + 1) * IMG]


def caption_grads(coefficient, images, outs, before_ref=None):
    for start in range(0, 2 * W, 256):
        columns = slice(start, start + 256)
        part = lax.dot_general(
            coefficient[...], images[columns, :], (((1,), (1,)), ((), ())),
            preferred_element_type=jnp.float32,
        )
        if before_ref is not None:
            part = part + before_ref[:, columns]
        rows = CAPS // len(outs)
        for i, out in enumerate(outs):
            out[:, columns] = part[i * rows : (i + 1) * rows]


def near_stage_kernel(
    place_ref, near_ref, far_ref, a_ref, b_ref,
    a_out, b_out, caption_out, captions_ref, turned_ref, images, tables, coefficient, sems,
):
    me = place_ref[0]
    copies = load_images(me & 1, (a_ref, b_ref), images, tables, sems)
    for e, ref in enumerate((near_ref, far_ref)):
        for j in range(4):
            for h in range(2):
                captions_ref[pl.ds((e * 4 + j) * HALF, HALF), h * W : (h + 1) * W] = ref[j, h]
    for block in range(2 * W // 128):
        columns = slice(block * 128, (block + 1) * 128)
        turned_ref[columns, :] = captions_ref[:, columns].T
    make_coefficients(0, me, captions_ref, images, tables, coefficient, copies)
    image_grads(me & 1, turned_ref, coefficient, a_out, b_out)
    caption_grads(coefficient, images, (caption_out,))


def far_stage_kernel(
    place_ref, captions_ref, turned_ref, a_ref, b_ref, before_ref,
    a_out, b_out, near_out, far_out, images, tables, coefficient, sems,
):
    me = place_ref[0]
    copies = load_images(me & 1, (a_ref, b_ref), images, tables, sems)
    make_coefficients(1, me, captions_ref, images, tables, coefficient, copies)
    image_grads(me & 1, turned_ref, coefficient, a_out, b_out)
    caption_grads(coefficient, images, (near_out, far_out), before_ref)


VMEM = pl.BlockSpec(memory_space=pltpu.VMEM)
SMEM = pl.BlockSpec(memory_space=pltpu.SMEM)
ANY = pl.BlockSpec(memory_space=pl.ANY)


def bf16(*shape):
    return jax.ShapeDtypeStruct(shape, jnp.bfloat16)


def f32(*shape):
    return jax.ShapeDtypeStruct(shape, jnp.float32)


def call(kernel, outs, ins, scratch=(), megabytes=8, flops=0, nbytes=1_000_000, **kwargs):
    return pl.pallas_call(
        kernel,
        out_shape=outs,
        in_specs=ins,
        out_specs=tuple(VMEM for _ in outs),
        scratch_shapes=list(scratch),
        compiler_params=pltpu.CompilerParams(vmem_limit_bytes=megabytes * 1024 * 1024),
        cost_estimate=pl.CostEstimate(flops=flops, bytes_accessed=nbytes, transcendentals=0),
        **kwargs,
    )


STAGE_SCRATCH = [
    pltpu.VMEM((2 * W, COLS), jnp.bfloat16),
    pltpu.VMEM((2, 4, 16, IMG), jnp.bfloat16),
    pltpu.VMEM((CAPS, COLS), jnp.bfloat16),
    pltpu.SemaphoreType.DMA((2, 8)),
]
DOT_FLOPS = 2 * CAPS * COLS * 2 * W


def body(image_emb, caption_emb, caption_count, caption_owner, pair_image):
    me = lax.axis_index("dp")
    xl = lax.axis_index("mp")
    place = me[None]

    extra = jnp.concatenate(
        [caption_count[None], pair_image.reshape(2, IMG), jnp.zeros((13, IMG), jnp.int32)], axis=0
    ).astype(jnp.bfloat16)
    piece = jnp.concatenate([image_emb.T, extra], axis=0)

    positions = jnp.arange(LOAD, dtype=jnp.int32)
    earlier = positions[None, :] < positions[:, None]
    same_owner = caption_owner[:, None] == caption_owner[None, :]
    rank = jnp.sum((same_owner & earlier).astype(jnp.int32), axis=1)
    marks = jnp.stack([caption_owner, me * 4 + rank], axis=1).astype(jnp.bfloat16)
    rows = jnp.concatenate([caption_emb, marks, jnp.zeros((LOAD, W - F - 2), jnp.bfloat16)], axis=1)
    kept = lax.dynamic_slice_in_dim(rows, xl * HALF, HALF, 0)
    given = lax.dynamic_slice_in_dim(rows, (1 - xl) * HALF, HALF, 0)

    received = [exchange(piece, first_axis(j)) for j in (1, 2, 3)]
    gained = exchange(given, other_half)
    pieces, pair = call(
        join_kernel, (bf16(4, ROWS, IMG), bf16(2, HALF, W)), [VMEM] * 6
    )(piece, *received, kept, gained)

    groups = [pieces] + [exchange(pieces, second_axis(j)) for j in (1, 2, 3)]
    (near,) = call(near_kernel, (bf16(4, 2, HALF, W),), [VMEM] * 4 + [ANY] * 2)(
        pair, *[exchange(pair, along_z(j)) for j in (1, 2, 3)], groups[1], groups[3]
    )
    far = exchange(near, other_core)
    half = jnp.float16
    image_own, image_1, caption_near, captions, turned = call(
        near_stage_kernel,
        (f32(4, F, IMG), f32(4, F, IMG), f32(CAPS, 2 * W), bf16(CAPS, 2 * W), bf16(2 * W, CAPS)),
        [SMEM, VMEM, VMEM, ANY, ANY],
        scratch=STAGE_SCRATCH, megabytes=10, flops=3 * DOT_FLOPS, nbytes=8_000_000,
    )(place, near, far, groups[0], groups[1])
    image_2, image_3, caption_own, caption_far = call(
        far_stage_kernel,
        (f32(4, F, IMG), f32(4, F, IMG), f32(CAPS // 2, 2 * W), f32(CAPS // 2, 2 * W)),
        [SMEM, VMEM, VMEM, ANY, ANY, VMEM],
        scratch=STAGE_SCRATCH, megabytes=10, flops=3 * DOT_FLOPS, nbytes=8_000_000,
    )(place, captions, turned, groups[2], groups[3], caption_near)
    crossed = exchange(caption_far, other_core)
    image_received = [
        exchange(image_1.astype(half), second_axis(1)),
        exchange(image_2.astype(half), second_axis(2)),
        exchange(image_3.astype(half), second_axis(3)),
    ]
    group_total = (caption_own + crossed).reshape(4, HALF, 2 * W)
    caption_received = [
        exchange(group_total[j].astype(half), along_z(j)) for j in (2, 1, 3)
    ]
    line = image_own
    for value in image_received:
        line = line + value.astype(jnp.float32)
    line_received = [exchange(line[j].astype(half), first_axis(j)) for j in (2, 1, 3)]
    total = line[0]
    for value in line_received:
        total = total + value.astype(jnp.float32)
    image_grad = total.astype(jnp.bfloat16).T

    both = group_total[0]
    for value in caption_received:
        both = both + value.astype(jnp.float32)
    both = both.astype(jnp.bfloat16)
    mine, theirs = both[:, :F], both[:, W : W + F]
    returned = exchange(theirs, other_half)
    caption_grad = jnp.where(
        xl == 0,
        jnp.concatenate([mine, returned], axis=0),
        jnp.concatenate([returned, mine], axis=0),
    )
    return image_grad, caption_grad


def solution(mesh):
    in_specs = (P("dp", "mp"), P("dp", "mp"), P("dp"), P("dp"), P("dp"))
    out_specs = (P("dp", "mp"), P("dp", "mp"))
    return jax.shard_map(body, mesh=mesh, in_specs=in_specs, out_specs=out_specs, check_vma=False)
```

```python
import functools

import jax
import jax.numpy as jnp
from jax import lax
from jax.experimental import pallas as pl
from jax.experimental.pallas import tpu as pltpu
from jax.sharding import PartitionSpec as P


F = 576
W = 640
IMG = 128
ROWS = F + 16
LOAD = 192
HALF = 96
CAPS = 8 * HALF
COLS = 4 * IMG


def exchange(value, move):
    pairs = []
    for source in range(128):
        xl, c, z, y, xh = source & 1, source >> 1 & 1, source >> 2 & 3, source >> 4 & 3, source >> 6
        jx, jy, jz, jc = move(c)
        x = (xh * 2 + xl) ^ jx
        target = ((((x >> 1) * 4 + (y ^ jy)) * 4 + (z ^ jz)) * 2 + (c ^ jc)) * 2 + (x & 1)
        pairs.append((source, target))
    return lax.ppermute(value, ("dp", "mp"), pairs)


def first_axis(j):
    return lambda c: (j, 0, 0, 0) if c == 0 else (0, j, 0, 0)


def second_axis(j):
    return lambda c: (0, j, 0, 0) if c == 0 else (j, 0, 0, 0)


def along_z(j):
    return lambda c: (0, 0, j, 0)


def other_half(c):
    return (1, 0, 0, 0)


def other_core(c):
    return (0, 0, 0, 1)


def join_kernel(piece_ref, r1_ref, r2_ref, r3_ref, kept_ref, gained_ref, pieces_ref, pair_ref):
    for i, ref in enumerate((piece_ref, r1_ref, r2_ref, r3_ref)):
        pieces_ref[i] = ref[...]
    pair_ref[0] = kept_ref[...]
    pair_ref[1, :, :F] = gained_ref[...]
    pair_ref[1, :, F:] = jnp.zeros((HALF, W - F), jnp.bfloat16)


def near_kernel(pair_ref, r1_ref, r2_ref, r3_ref, _a, _b, near_ref):
    for i, ref in enumerate((pair_ref, r1_ref, r2_ref, r3_ref)):
        near_ref[i] = ref[...]


def load_images(c, refs, images, tables, sems):
    copies = []
    for low, ref in enumerate(refs):
        for p1 in range(4):
            h = jnp.where(c == 0, p1 & 1, low)
            q = jnp.where(c == 0, low * 2 + (p1 >> 1), p1)
            copies.append(
                pltpu.make_async_copy(
                    ref.at[p1, pl.ds(0, F)],
                    images.at[pl.ds(pl.multiple_of(h * F, F), F), pl.ds(pl.multiple_of(q * IMG, IMG), IMG)],
                    sems.at[0, low * 4 + p1],
                )
            )
            copies.append(
                pltpu.make_async_copy(
                    ref.at[p1, pl.ds(F, 16)], tables.at[h, q], sems.at[1, low * 4 + p1]
                )
            )
    for copy in copies:
        copy.start()
    return copies


def make_coefficients(stage, me, captions_ref, marks_ref, images, tables, coefficient, copies):
    c = me & 1
    marks = marks_ref[...].astype(jnp.float32).astype(jnp.int32)
    owner, slot = marks[:, 64:65], marks[:, 65:66]
    relative = owner ^ me
    near_y, near_x = relative >> 3 & 3, relative >> 5
    column = jnp.where(c == 0, near_y * 2 + near_x, near_x * 4 + near_y) - 4 * stage
    picked = (lax.broadcasted_iota(jnp.int32, (CAPS, 256), 1) == slot).astype(jnp.float32)
    for copy in copies:
        copy.wait()

    table = tables[0].astype(jnp.float32)
    inverse = 1.0 / table[:, 0, :]
    slots = jnp.concatenate([table[:, 1, :], table[:, 2, :]], axis=1)
    slots = jnp.concatenate([slots, jnp.zeros((124, 256), jnp.float32)], axis=0)
    named = lax.dot_general(
        picked.astype(jnp.bfloat16), slots.astype(jnp.bfloat16), (((1,), (1,)), ((), ())),
        preferred_element_type=jnp.float32,
    )
    lanes = lax.broadcasted_iota(jnp.int32, (CAPS, 128), 1)
    named = jnp.sum(jnp.where(lanes == column, named, 0.0), axis=1, keepdims=True)
    inside = ((relative & 7) == 0) & (column >= 0) & (column < 4)
    target = jnp.where(inside, column * IMG + named.astype(jnp.int32), -1)

    for u in range(2):
        columns = slice(u * 256, (u + 1) * 256)
        products = jnp.dot(
            captions_ref[...], images[:, columns], preferred_element_type=jnp.float32
        )
        negative = 5.0 * jnp.tanh(5.0 * products - 1.0) + 5.0
        weight = jnp.concatenate([inverse[2 * u : 2 * u + 1], inverse[2 * u + 1 : 2 * u + 2]], axis=1)
        here = lax.broadcasted_iota(jnp.int32, (CAPS, 256), 1) + u * 256 == target
        part = jnp.where(here, weight * (negative - 10.0), negative)
        coefficient[:, columns] = part.astype(jnp.bfloat16)


def image_grads(c, turned_ref, coefficient, a_out, b_out):
    for low, out in enumerate((a_out, b_out)):
        for t in range(2):
            u = jnp.where(c == 0, low, t)
            h = jnp.where(c == 0, t, low)
            grads = jnp.dot(
                turned_ref[pl.ds(pl.multiple_of(h * F, F), F), :],
                coefficient[:, pl.ds(pl.multiple_of(u * 256, 256), 256)],
                preferred_element_type=jnp.float32,
            )
            for g in range(2):
                p1 = jnp.where(c == 0, g * 2 + t, t * 2 + g)
                out[p1] = grads[:, g * IMG : (g + 1) * IMG]


def caption_grads(coefficient, images, outs, before_ref=None):
    for start in range(0, 2 * F, 256):
        columns = slice(start, min(start + 256, 2 * F))
        part = lax.dot_general(
            coefficient[...], images[columns, :], (((1,), (1,)), ((), ())),
            preferred_element_type=jnp.float32,
        )
        if before_ref is not None:
            part = part + before_ref[:, columns]
        rows = CAPS // len(outs)
        for i, out in enumerate(outs):
            out[:, columns] = part[i * rows : (i + 1) * rows]


def near_stage_kernel(
    place_ref, near_ref, far_ref, a_ref, b_ref,
    a_out, b_out, caption_out, captions_ref, turned_ref, marks_ref, images, tables, coefficient, sems,
):
    me = place_ref[0]
    copies = load_images(me & 1, (a_ref, b_ref), images, tables, sems)
    for e, ref in enumerate((near_ref, far_ref)):
        for j in range(4):
            for h in range(2):
                rows = pl.ds((e * 4 + j) * HALF, HALF)
                captions_ref[rows, h * F : (h + 1) * F] = ref[j, h, :, :F]
                if h == 0:
                    marks_ref[rows, :] = ref[j, 0, :, 512:640]
    for block in range(2 * F // 128):
        columns = slice(block * 128, (block + 1) * 128)
        turned_ref[columns, :] = captions_ref[:, columns].T
    make_coefficients(0, me, captions_ref, marks_ref, images, tables, coefficient, copies)
    image_grads(me & 1, turned_ref, coefficient, a_out, b_out)
    caption_grads(coefficient, images, (caption_out,))


def far_stage_kernel(
    place_ref, captions_ref, turned_ref, marks_ref, a_ref, b_ref, before_ref,
    a_out, b_out, near_out, far_out, images, tables, coefficient, sems,
):
    me = place_ref[0]
    copies = load_images(me & 1, (a_ref, b_ref), images, tables, sems)
    make_coefficients(1, me, captions_ref, marks_ref, images, tables, coefficient, copies)
    image_grads(me & 1, turned_ref, coefficient, a_out, b_out)
    caption_grads(coefficient, images, (near_out, far_out), before_ref)


VMEM = pl.BlockSpec(memory_space=pltpu.VMEM)
SMEM = pl.BlockSpec(memory_space=pltpu.SMEM)
ANY = pl.BlockSpec(memory_space=pl.ANY)


def bf16(*shape):
    return jax.ShapeDtypeStruct(shape, jnp.bfloat16)


def f32(*shape):
    return jax.ShapeDtypeStruct(shape, jnp.float32)


def call(kernel, outs, ins, scratch=(), megabytes=8, flops=0, nbytes=1_000_000, **kwargs):
    return pl.pallas_call(
        kernel,
        out_shape=outs,
        in_specs=ins,
        out_specs=tuple(VMEM for _ in outs),
        scratch_shapes=list(scratch),
        compiler_params=pltpu.CompilerParams(vmem_limit_bytes=megabytes * 1024 * 1024),
        cost_estimate=pl.CostEstimate(flops=flops, bytes_accessed=nbytes, transcendentals=0),
        **kwargs,
    )


STAGE_SCRATCH = [
    pltpu.VMEM((2 * F, COLS), jnp.bfloat16),
    pltpu.VMEM((2, 4, 16, IMG), jnp.bfloat16),
    pltpu.VMEM((CAPS, COLS), jnp.bfloat16),
    pltpu.SemaphoreType.DMA((2, 8)),
]
DOT_FLOPS = 2 * CAPS * COLS * 2 * F


def after(values, earlier):
    return lax.optimization_barrier((values, earlier))[0]


def body(image_emb, caption_emb, caption_count, caption_owner, pair_image):
    me = lax.axis_index("dp")
    xl = lax.axis_index("mp")
    place = me[None]

    given = lax.dynamic_slice_in_dim(caption_emb, (1 - xl) * HALF, HALF, 0)
    gained = exchange(given, other_half)
    extra = lax.optimization_barrier(
        jnp.concatenate(
            [caption_count[None], pair_image.reshape(2, IMG), jnp.zeros((13, IMG), jnp.int32)], axis=0
        )
    )
    piece = jnp.concatenate([image_emb.T, extra.astype(jnp.bfloat16)], axis=0)

    received = [exchange(piece, first_axis(j)) for j in (1, 2, 3)]
    positions = jnp.arange(LOAD, dtype=jnp.int32)
    earlier = positions[None, :] < positions[:, None]
    same_owner = caption_owner[:, None] == caption_owner[None, :]
    rank = jnp.sum((same_owner & earlier).astype(jnp.int32), axis=1)
    marks = jnp.stack([caption_owner, me * 4 + rank], axis=1).astype(jnp.bfloat16)
    rows = jnp.concatenate([caption_emb, marks, jnp.zeros((LOAD, W - F - 2), jnp.bfloat16)], axis=1)
    kept = lax.dynamic_slice_in_dim(rows, xl * HALF, HALF, 0)
    pieces, pair = call(
        join_kernel, (bf16(4, ROWS, IMG), bf16(2, HALF, W)), [VMEM] * 6
    )(piece, *received, kept, gained)

    groups = [pieces] + [exchange(pieces, second_axis(j)) for j in (1, 2, 3)]
    (near,) = call(near_kernel, (bf16(4, 2, HALF, W),), [VMEM] * 4 + [ANY] * 2)(
        pair, *[exchange(pair, along_z(j)) for j in (1, 2, 3)], groups[1], groups[3]
    )
    far = exchange(near, other_core)
    half = jnp.float16
    image_own, image_1, caption_near, captions, turned, marks = call(
        near_stage_kernel,
        (
            f32(4, F, IMG), f32(4, F, IMG), f32(CAPS, 2 * F),
            bf16(CAPS, 2 * F), bf16(2 * F, CAPS), bf16(CAPS, 128),
        ),
        [SMEM, VMEM, VMEM, ANY, ANY],
        scratch=STAGE_SCRATCH, megabytes=10, flops=3 * DOT_FLOPS, nbytes=8_000_000,
    )(place, near, far, groups[0], groups[1])
    image_1 = image_1.astype(half)
    received_1 = exchange(image_1, second_axis(1))
    caption_near = after(caption_near, image_1)
    image_2, image_3, caption_own, caption_far = call(
        far_stage_kernel,
        (f32(4, F, IMG), f32(4, F, IMG), f32(CAPS // 2, 2 * F), f32(CAPS // 2, 2 * F)),
        [SMEM, VMEM, VMEM, VMEM, ANY, ANY, VMEM],
        scratch=STAGE_SCRATCH, megabytes=10, flops=3 * DOT_FLOPS, nbytes=8_000_000,
    )(place, captions, turned, marks, groups[2], groups[3], caption_near)
    image_2, image_3 = image_2.astype(half), image_3.astype(half)
    caption_far = after(caption_far, (received_1, image_2, image_3)).astype(half)
    crossed = exchange(caption_far, other_core)
    image_received = [
        received_1,
        exchange(image_2, second_axis(2)),
        exchange(image_3, second_axis(3)),
    ]
    group_total = (caption_own + crossed.astype(jnp.float32)).reshape(4, HALF, 2 * F)
    messages = [group_total[j].astype(half) for j in (2, 1, 3)]
    caption_received = [exchange(m, along_z(j)) for m, j in zip(messages, (2, 1, 3))]
    image_received = after(image_received, messages)
    line = image_own
    for value in image_received:
        line = line + value.astype(jnp.float32)
    line_received = [exchange(line[j].astype(half), first_axis(j)) for j in (2, 1, 3)]
    total = line[0]
    for value in line_received:
        total = total + value.astype(jnp.float32)
    image_grad = total.astype(jnp.bfloat16).T

    both = group_total[0]
    for value in caption_received:
        both = both + value.astype(jnp.float32)
    both = both.astype(jnp.bfloat16)
    mine, theirs = both[:, :F], both[:, F:]
    returned = exchange(theirs, other_half)
    caption_grad = jnp.where(
        xl == 0,
        jnp.concatenate([mine, returned], axis=0),
        jnp.concatenate([returned, mine], axis=0),
    )
    return image_grad, caption_grad


def solution(mesh):
    in_specs = (P("dp", "mp"), P("dp", "mp"), P("dp"), P("dp"), P("dp"))
    out_specs = (P("dp", "mp"), P("dp", "mp"))
    return jax.shard_map(body, mesh=mesh, in_specs=in_specs, out_specs=out_specs, check_vma=False)
```

```python
import functools

import jax
import jax.numpy as jnp
from jax import lax
from jax.experimental import pallas as pl
from jax.experimental.pallas import tpu as pltpu
from jax.sharding import PartitionSpec as P


F = 576
W = 640
IMG = 128
ROWS = F + 16
LOAD = 192
HALF = 96
CAPS = 8 * HALF
COLS = 4 * IMG


def exchange(value, move):
    pairs = []
    for source in range(128):
        xl, c, z, y, xh = source & 1, source >> 1 & 1, source >> 2 & 3, source >> 4 & 3, source >> 6
        jx, jy, jz, jc = move(c)
        x = (xh * 2 + xl) ^ jx
        target = ((((x >> 1) * 4 + (y ^ jy)) * 4 + (z ^ jz)) * 2 + (c ^ jc)) * 2 + (x & 1)
        pairs.append((source, target))
    return lax.ppermute(value, ("dp", "mp"), pairs)


def first_axis(j):
    return lambda c: (j, 0, 0, 0) if c == 0 else (0, j, 0, 0)


def second_axis(j):
    return lambda c: (0, j, 0, 0) if c == 0 else (j, 0, 0, 0)


def along_z(j):
    return lambda c: (0, 0, j, 0)


def other_half(c):
    return (1, 0, 0, 0)


def other_core(c):
    return (0, 0, 0, 1)


def join_kernel(piece_ref, r1_ref, r2_ref, r3_ref, kept_ref, gained_ref, pieces_ref, pair_ref):
    for i, ref in enumerate((piece_ref, r1_ref, r2_ref, r3_ref)):
        pieces_ref[i] = ref[...]
    pair_ref[0] = kept_ref[...]
    pair_ref[1, :, :F] = gained_ref[...]
    pair_ref[1, :, F:] = jnp.zeros((HALF, W - F), jnp.bfloat16)


def near_kernel(pair_ref, r1_ref, r2_ref, r3_ref, _a, _b, near_ref):
    for i, ref in enumerate((pair_ref, r1_ref, r2_ref, r3_ref)):
        near_ref[i] = ref[...]


def load_images(c, refs, images, tables, sems):
    copies = []
    for low, ref in enumerate(refs):
        for p1 in range(4):
            h = jnp.where(c == 0, p1 & 1, low)
            q = jnp.where(c == 0, low * 2 + (p1 >> 1), p1)
            copies.append(
                pltpu.make_async_copy(
                    ref.at[p1, pl.ds(0, F)],
                    images.at[pl.ds(pl.multiple_of(h * F, F), F), pl.ds(pl.multiple_of(q * IMG, IMG), IMG)],
                    sems.at[0, low * 4 + p1],
                )
            )
            copies.append(
                pltpu.make_async_copy(
                    ref.at[p1, pl.ds(F, 16)], tables.at[h, q], sems.at[1, low * 4 + p1]
                )
            )
    for copy in copies:
        copy.start()
    return copies


def make_coefficients(stage, me, captions_ref, marks_ref, images, tables, coefficient, copies):
    c = me & 1
    marks = marks_ref[...].astype(jnp.float32).astype(jnp.int32)
    owner, slot = marks[:, 64:65], marks[:, 65:66]
    relative = owner ^ me
    near_y, near_x = relative >> 3 & 3, relative >> 5
    column = jnp.where(c == 0, near_y * 2 + near_x, near_x * 4 + near_y) - 4 * stage
    picked = (lax.broadcasted_iota(jnp.int32, (CAPS, 256), 1) == slot).astype(jnp.float32)
    for copy in copies:
        copy.wait()

    table = tables[0].astype(jnp.float32)
    inverse = 1.0 / table[:, 0, :]
    slots = jnp.concatenate([table[:, 1, :], table[:, 2, :]], axis=1)
    slots = jnp.concatenate([slots, jnp.zeros((124, 256), jnp.float32)], axis=0)
    named = lax.dot_general(
        picked.astype(jnp.bfloat16), slots.astype(jnp.bfloat16), (((1,), (1,)), ((), ())),
        preferred_element_type=jnp.float32,
    )
    lanes = lax.broadcasted_iota(jnp.int32, (CAPS, 128), 1)
    named = jnp.sum(jnp.where(lanes == column, named, 0.0), axis=1, keepdims=True)
    inside = ((relative & 7) == 0) & (column >= 0) & (column < 4)
    target = jnp.where(inside, column * IMG + named.astype(jnp.int32), -1)

    for u in range(2):
        columns = slice(u * 256, (u + 1) * 256)
        products = jnp.dot(
            captions_ref[...], images[:, columns], preferred_element_type=jnp.float32
        )
        negative = 5.0 * jnp.tanh(5.0 * products - 1.0) + 5.0
        weight = jnp.concatenate([inverse[2 * u : 2 * u + 1], inverse[2 * u + 1 : 2 * u + 2]], axis=1)
        here = lax.broadcasted_iota(jnp.int32, (CAPS, 256), 1) + u * 256 == target
        part = jnp.where(here, weight * (negative - 10.0), negative)
        coefficient[:, columns] = part.astype(jnp.bfloat16)


def image_grads(c, turned_ref, coefficient, a_out, b_out):
    for low, out in enumerate((a_out, b_out)):
        for t in range(2):
            u = jnp.where(c == 0, low, t)
            h = jnp.where(c == 0, t, low)
            grads = jnp.dot(
                turned_ref[pl.ds(pl.multiple_of(h * F, F), F), :],
                coefficient[:, pl.ds(pl.multiple_of(u * 256, 256), 256)],
                preferred_element_type=jnp.float32,
            )
            for g in range(2):
                p1 = jnp.where(c == 0, g * 2 + t, t * 2 + g)
                out[p1] = grads[:, g * IMG : (g + 1) * IMG]


def caption_grads(coefficient, images, outs, before_ref=None):
    for start in range(0, 2 * F, 256):
        columns = slice(start, min(start + 256, 2 * F))
        part = lax.dot_general(
            coefficient[...], images[columns, :], (((1,), (1,)), ((), ())),
            preferred_element_type=jnp.float32,
        )
        if before_ref is not None:
            part = part + before_ref[:, columns]
        rows = CAPS // len(outs)
        for i, out in enumerate(outs):
            out[:, columns] = part[i * rows : (i + 1) * rows]


def near_stage_kernel(
    place_ref, near_ref, far_ref, a_ref, b_ref,
    a_out, b_out, caption_out, captions_ref, turned_ref, marks_ref, images, tables, coefficient, sems,
):
    me = place_ref[0]
    copies = load_images(me & 1, (a_ref, b_ref), images, tables, sems)
    for e, ref in enumerate((near_ref, far_ref)):
        for j in range(4):
            for h in range(2):
                rows = pl.ds((e * 4 + j) * HALF, HALF)
                captions_ref[rows, h * F : (h + 1) * F] = ref[j, h, :, :F]
                if h == 0:
                    marks_ref[rows, :] = ref[j, 0, :, 512:640]
    for block in range(2 * F // 128):
        columns = slice(block * 128, (block + 1) * 128)
        turned_ref[columns, :] = captions_ref[:, columns].T
    make_coefficients(0, me, captions_ref, marks_ref, images, tables, coefficient, copies)
    image_grads(me & 1, turned_ref, coefficient, a_out, b_out)
    caption_grads(coefficient, images, (caption_out,))


def far_stage_kernel(
    place_ref, captions_ref, turned_ref, marks_ref, a_ref, b_ref, before_ref,
    a_out, b_out, near_out, far_out, images, tables, coefficient, sems,
):
    me = place_ref[0]
    copies = load_images(me & 1, (a_ref, b_ref), images, tables, sems)
    make_coefficients(1, me, captions_ref, marks_ref, images, tables, coefficient, copies)
    image_grads(me & 1, turned_ref, coefficient, a_out, b_out)
    caption_grads(coefficient, images, (near_out, far_out), before_ref)


VMEM = pl.BlockSpec(memory_space=pltpu.VMEM)
SMEM = pl.BlockSpec(memory_space=pltpu.SMEM)
ANY = pl.BlockSpec(memory_space=pl.ANY)


def bf16(*shape):
    return jax.ShapeDtypeStruct(shape, jnp.bfloat16)


def f32(*shape):
    return jax.ShapeDtypeStruct(shape, jnp.float32)


def call(kernel, outs, ins, scratch=(), megabytes=8, flops=0, nbytes=1_000_000, **kwargs):
    return pl.pallas_call(
        kernel,
        out_shape=outs,
        in_specs=ins,
        out_specs=tuple(VMEM for _ in outs),
        scratch_shapes=list(scratch),
        compiler_params=pltpu.CompilerParams(vmem_limit_bytes=megabytes * 1024 * 1024),
        cost_estimate=pl.CostEstimate(flops=flops, bytes_accessed=nbytes, transcendentals=0),
        **kwargs,
    )


STAGE_SCRATCH = [
    pltpu.VMEM((2 * F, COLS), jnp.bfloat16),
    pltpu.VMEM((2, 4, 16, IMG), jnp.bfloat16),
    pltpu.VMEM((CAPS, COLS), jnp.bfloat16),
    pltpu.SemaphoreType.DMA((2, 8)),
]
DOT_FLOPS = 2 * CAPS * COLS * 2 * F


def after(values, earlier):
    return lax.optimization_barrier((values, earlier))[0]


def body(image_emb, caption_emb, caption_count, caption_owner, pair_image):
    me = lax.axis_index("dp")
    xl = lax.axis_index("mp")
    place = me[None]

    given = lax.dynamic_slice_in_dim(caption_emb, (1 - xl) * HALF, HALF, 0)
    gained = exchange(given, other_half)
    extra = lax.optimization_barrier(
        jnp.concatenate(
            [caption_count[None], pair_image.reshape(2, IMG), jnp.zeros((13, IMG), jnp.int32)], axis=0
        )
    )
    piece = jnp.concatenate([image_emb.T, extra.astype(jnp.bfloat16)], axis=0)

    received = [exchange(piece, first_axis(j)) for j in (1, 2, 3)]
    positions = jnp.arange(LOAD, dtype=jnp.int32)
    earlier = positions[None, :] < positions[:, None]
    same_owner = caption_owner[:, None] == caption_owner[None, :]
    rank = jnp.sum((same_owner & earlier).astype(jnp.int32), axis=1)
    marks = jnp.stack([caption_owner, me * 4 + rank], axis=1).astype(jnp.bfloat16)
    rows = jnp.concatenate([caption_emb, marks, jnp.zeros((LOAD, W - F - 2), jnp.bfloat16)], axis=1)
    kept = lax.dynamic_slice_in_dim(rows, xl * HALF, HALF, 0)
    pieces, pair = call(
        join_kernel, (bf16(4, ROWS, IMG), bf16(2, HALF, W)), [VMEM] * 6
    )(piece, *received, kept, gained)

    groups = [pieces] + [exchange(pieces, second_axis(j)) for j in (1, 2, 3)]
    (near,) = call(near_kernel, (bf16(4, 2, HALF, W),), [VMEM] * 4 + [ANY] * 2)(
        pair, *[exchange(pair, along_z(j)) for j in (1, 2, 3)], groups[1], groups[3]
    )
    far = exchange(near, other_core)
    half = jnp.float16
    image_own, image_1, caption_near, captions, turned, marks = call(
        near_stage_kernel,
        (
            f32(4, F, IMG), f32(4, F, IMG), f32(CAPS, 2 * F),
            bf16(CAPS, 2 * F), bf16(2 * F, CAPS), bf16(CAPS, 128),
        ),
        [SMEM, VMEM, VMEM, ANY, ANY],
        scratch=STAGE_SCRATCH, megabytes=10, flops=3 * DOT_FLOPS, nbytes=8_000_000,
    )(place, near, far, groups[0], groups[1])
    image_1 = image_1.astype(half)
    received_1 = exchange(image_1, second_axis(1))
    caption_near = after(caption_near, image_1)
    image_2, image_3, caption_own, caption_far = call(
        far_stage_kernel,
        (f32(4, F, IMG), f32(4, F, IMG), f32(CAPS // 2, 2 * F), f32(CAPS // 2, 2 * F)),
        [SMEM, VMEM, VMEM, VMEM, ANY, ANY, VMEM],
        scratch=STAGE_SCRATCH, megabytes=10, flops=3 * DOT_FLOPS, nbytes=8_000_000,
    )(place, captions, turned, marks, groups[2], groups[3], caption_near)
    image_2, image_3 = image_2.astype(half), image_3.astype(half)
    caption_far = after(caption_far, (received_1, image_2, image_3)).astype(half)
    crossed = exchange(caption_far, other_core)
    image_received = [
        received_1,
        exchange(image_2, second_axis(2)),
        exchange(image_3, second_axis(3)),
    ]
    group_total = (caption_own + crossed.astype(jnp.float32)).reshape(4, HALF, 2 * F)
    messages = [group_total[j].astype(half) for j in (2, 1, 3)]
    caption_received = [exchange(m, along_z(j)) for m, j in zip(messages, (2, 1, 3))]
    image_received = after(image_received, messages)
    line = image_own
    for value in image_received:
        line = line + value.astype(jnp.float32)
    both = group_total[0]
    for value in caption_received:
        both = both + value.astype(jnp.float32)
    both = both.astype(jnp.bfloat16)
    mine, theirs = both[:, :F], both[:, F:]
    returned = exchange(theirs, other_half)
    line = after(line, theirs)
    line_received = [exchange(line[j].astype(half), first_axis(j)) for j in (2, 1, 3)]
    total = line[0]
    for value in line_received:
        total = total + value.astype(jnp.float32)
    image_grad = total.astype(jnp.bfloat16).T

    caption_grad = jnp.where(
        xl == 0,
        jnp.concatenate([mine, returned], axis=0),
        jnp.concatenate([returned, mine], axis=0),
    )
    return image_grad, caption_grad


def solution(mesh):
    in_specs = (P("dp", "mp"), P("dp", "mp"), P("dp"), P("dp"), P("dp"))
    out_specs = (P("dp", "mp"), P("dp", "mp"))
    return jax.shard_map(body, mesh=mesh, in_specs=in_specs, out_specs=out_specs, check_vma=False)
```

```python
import functools

import jax
import jax.numpy as jnp
from jax import lax
from jax.experimental import pallas as pl
from jax.experimental.pallas import tpu as pltpu
from jax.sharding import PartitionSpec as P


F = 576
W = 640
IMG = 128
ROWS = F + 16
LOAD = 192
HALF = 96
CAPS = 8 * HALF
COLS = 4 * IMG


def exchange(value, move):
    pairs = []
    for source in range(128):
        xl, c, z, y, xh = source & 1, source >> 1 & 1, source >> 2 & 3, source >> 4 & 3, source >> 6
        jx, jy, jz, jc = move(c)
        x = (xh * 2 + xl) ^ jx
        target = ((((x >> 1) * 4 + (y ^ jy)) * 4 + (z ^ jz)) * 2 + (c ^ jc)) * 2 + (x & 1)
        pairs.append((source, target))
    return lax.ppermute(value, ("dp", "mp"), pairs)


def first_axis(j):
    return lambda c: (j, 0, 0, 0) if c == 0 else (0, j, 0, 0)


def second_axis(j):
    return lambda c: (0, j, 0, 0) if c == 0 else (j, 0, 0, 0)


def along_z(j):
    return lambda c: (0, 0, j, 0)


def other_half(c):
    return (1, 0, 0, 0)


def other_core(c):
    return (0, 0, 0, 1)


def join_kernel(piece_ref, r1_ref, r2_ref, r3_ref, kept_ref, gained_ref, pieces_ref, pair_ref):
    for i, ref in enumerate((piece_ref, r1_ref, r2_ref, r3_ref)):
        pieces_ref[i] = ref[...]
    pair_ref[0] = kept_ref[...]
    pair_ref[1, :, :F] = gained_ref[...]
    pair_ref[1, :, F:] = jnp.zeros((HALF, W - F), jnp.bfloat16)


def near_kernel(pair_ref, r1_ref, r2_ref, r3_ref, _a, _b, near_ref):
    for i, ref in enumerate((pair_ref, r1_ref, r2_ref, r3_ref)):
        near_ref[i] = ref[...]


def load_images(c, refs, images, tables, sems):
    copies = []
    for low, ref in enumerate(refs):
        for p1 in range(4):
            h = jnp.where(c == 0, p1 & 1, low)
            q = jnp.where(c == 0, low * 2 + (p1 >> 1), p1)
            copies.append(
                pltpu.make_async_copy(
                    ref.at[p1, pl.ds(0, F)],
                    images.at[pl.ds(pl.multiple_of(h * F, F), F), pl.ds(pl.multiple_of(q * IMG, IMG), IMG)],
                    sems.at[0, low * 4 + p1],
                )
            )
            copies.append(
                pltpu.make_async_copy(
                    ref.at[p1, pl.ds(F, 16)], tables.at[h, q], sems.at[1, low * 4 + p1]
                )
            )
    for copy in copies:
        copy.start()
    return copies


def make_coefficients(stage, me, captions_ref, marks_ref, images, tables, coefficient, copies):
    c = me & 1
    marks = marks_ref[...].astype(jnp.float32).astype(jnp.int32)
    owner, slot = marks[:, 64:65], marks[:, 65:66]
    relative = owner ^ me
    near_y, near_x = relative >> 3 & 3, relative >> 5
    column = jnp.where(c == 0, near_y * 2 + near_x, near_x * 4 + near_y) - 4 * stage
    picked = (lax.broadcasted_iota(jnp.int32, (CAPS, 256), 1) == slot).astype(jnp.float32)
    for copy in copies:
        copy.wait()

    table = tables[0].astype(jnp.float32)
    inverse = 1.0 / table[:, 0, :]
    slots = jnp.concatenate([table[:, 1, :], table[:, 2, :]], axis=1)
    slots = jnp.concatenate([slots, jnp.zeros((124, 256), jnp.float32)], axis=0)
    named = lax.dot_general(
        picked.astype(jnp.bfloat16), slots.astype(jnp.bfloat16), (((1,), (1,)), ((), ())),
        preferred_element_type=jnp.float32,
    )
    lanes = lax.broadcasted_iota(jnp.int32, (CAPS, 128), 1)
    named = jnp.sum(jnp.where(lanes == column, named, 0.0), axis=1, keepdims=True)
    inside = ((relative & 7) == 0) & (column >= 0) & (column < 4)
    target = jnp.where(inside, column * IMG + named.astype(jnp.int32), -1)

    for u in range(2):
        columns = slice(u * 256, (u + 1) * 256)
        products = jnp.dot(
            captions_ref[...], images[:, columns], preferred_element_type=jnp.float32
        )
        negative = 5.0 * jnp.tanh(5.0 * products - 1.0) + 5.0
        weight = jnp.concatenate([inverse[2 * u : 2 * u + 1], inverse[2 * u + 1 : 2 * u + 2]], axis=1)
        here = lax.broadcasted_iota(jnp.int32, (CAPS, 256), 1) + u * 256 == target
        part = jnp.where(here, weight * (negative - 10.0), negative)
        coefficient[:, columns] = part.astype(jnp.bfloat16)


def image_grads(c, turned_ref, coefficient, a_out, b_out):
    for low, out in enumerate((a_out, b_out)):
        for t in range(2):
            u = jnp.where(c == 0, low, t)
            h = jnp.where(c == 0, t, low)
            grads = jnp.dot(
                turned_ref[pl.ds(pl.multiple_of(h * F, F), F), :],
                coefficient[:, pl.ds(pl.multiple_of(u * 256, 256), 256)],
                preferred_element_type=jnp.float32,
            )
            for g in range(2):
                p1 = jnp.where(c == 0, g * 2 + t, t * 2 + g)
                out[p1] = grads[:, g * IMG : (g + 1) * IMG]


def caption_grads(coefficient, images, outs, before_ref=None):
    for start in range(0, 2 * F, 256):
        columns = slice(start, min(start + 256, 2 * F))
        part = lax.dot_general(
            coefficient[...], images[columns, :], (((1,), (1,)), ((), ())),
            preferred_element_type=jnp.float32,
        )
        if before_ref is not None:
            part = part + before_ref[:, columns]
        rows = CAPS // len(outs)
        for i, out in enumerate(outs):
            out[:, columns] = part[i * rows : (i + 1) * rows]


def near_stage_kernel(
    place_ref, near_ref, far_ref, a_ref, b_ref,
    a_out, b_out, caption_out, captions_ref, turned_ref, marks_ref, images, tables, coefficient, sems,
):
    me = place_ref[0]
    copies = load_images(me & 1, (a_ref, b_ref), images, tables, sems)
    for e, ref in enumerate((near_ref, far_ref)):
        for j in range(4):
            for h in range(2):
                rows = pl.ds((e * 4 + j) * HALF, HALF)
                captions_ref[rows, h * F : (h + 1) * F] = ref[j, h, :, :F]
                if h == 0:
                    marks_ref[rows, :] = ref[j, 0, :, 512:640]
    for block in range(2 * F // 128):
        columns = slice(block * 128, (block + 1) * 128)
        turned_ref[columns, :] = captions_ref[:, columns].T
    make_coefficients(0, me, captions_ref, marks_ref, images, tables, coefficient, copies)
    image_grads(me & 1, turned_ref, coefficient, a_out, b_out)
    caption_grads(coefficient, images, (caption_out,))


def far_stage_kernel(
    place_ref, captions_ref, turned_ref, marks_ref, a_ref, b_ref, before_ref,
    a_out, b_out, near_out, far_out, images, tables, coefficient, sems,
):
    me = place_ref[0]
    copies = load_images(me & 1, (a_ref, b_ref), images, tables, sems)
    make_coefficients(1, me, captions_ref, marks_ref, images, tables, coefficient, copies)
    image_grads(me & 1, turned_ref, coefficient, a_out, b_out)
    caption_grads(coefficient, images, (near_out, far_out), before_ref)


VMEM = pl.BlockSpec(memory_space=pltpu.VMEM)
SMEM = pl.BlockSpec(memory_space=pltpu.SMEM)
ANY = pl.BlockSpec(memory_space=pl.ANY)


def bf16(*shape):
    return jax.ShapeDtypeStruct(shape, jnp.bfloat16)


def f32(*shape):
    return jax.ShapeDtypeStruct(shape, jnp.float32)


def call(kernel, outs, ins, scratch=(), megabytes=8, flops=0, nbytes=1_000_000, **kwargs):
    return pl.pallas_call(
        kernel,
        out_shape=outs,
        in_specs=ins,
        out_specs=tuple(VMEM for _ in outs),
        scratch_shapes=list(scratch),
        compiler_params=pltpu.CompilerParams(vmem_limit_bytes=megabytes * 1024 * 1024),
        cost_estimate=pl.CostEstimate(flops=flops, bytes_accessed=nbytes, transcendentals=0),
        **kwargs,
    )


STAGE_SCRATCH = [
    pltpu.VMEM((2 * F, COLS), jnp.bfloat16),
    pltpu.VMEM((2, 4, 16, IMG), jnp.bfloat16),
    pltpu.VMEM((CAPS, COLS), jnp.bfloat16),
    pltpu.SemaphoreType.DMA((2, 8)),
]
DOT_FLOPS = 2 * CAPS * COLS * 2 * F


def after(values, earlier):
    return lax.optimization_barrier((values, earlier))[0]


def body(image_emb, caption_emb, caption_count, caption_owner, pair_image):
    me = lax.axis_index("dp")
    xl = lax.axis_index("mp")
    place = me[None]

    given = lax.dynamic_slice_in_dim(caption_emb, (1 - xl) * HALF, HALF, 0)
    gained = exchange(given, other_half)
    extra = lax.optimization_barrier(
        jnp.concatenate(
            [caption_count[None], pair_image.reshape(2, IMG), jnp.zeros((13, IMG), jnp.int32)], axis=0
        )
    )
    piece = jnp.concatenate([image_emb.T, extra.astype(jnp.bfloat16)], axis=0)

    received = [exchange(piece, first_axis(j)) for j in (1, 2, 3)]
    positions = jnp.arange(LOAD, dtype=jnp.int32)
    earlier = positions[None, :] < positions[:, None]
    same_owner = caption_owner[:, None] == caption_owner[None, :]
    rank = jnp.sum((same_owner & earlier).astype(jnp.int32), axis=1)
    marks = jnp.stack([caption_owner, me * 4 + rank], axis=1).astype(jnp.bfloat16)
    rows = jnp.concatenate([caption_emb, marks, jnp.zeros((LOAD, W - F - 2), jnp.bfloat16)], axis=1)
    kept = lax.dynamic_slice_in_dim(rows, xl * HALF, HALF, 0)
    pieces, pair = call(
        join_kernel, (bf16(4, ROWS, IMG), bf16(2, HALF, W)), [VMEM] * 6
    )(piece, *received, kept, gained)

    groups = [pieces] + [exchange(pieces, second_axis(j)) for j in (1, 2, 3)]
    (near,) = call(near_kernel, (bf16(4, 2, HALF, W),), [VMEM] * 4 + [ANY] * 2)(
        pair, *[exchange(pair, along_z(j)) for j in (1, 2, 3)], groups[1], groups[3]
    )
    far = exchange(near, other_core)
    half = jnp.float16
    image_own, image_1, caption_near, captions, turned, marks = call(
        near_stage_kernel,
        (
            f32(4, F, IMG), f32(4, F, IMG), f32(CAPS, 2 * F),
            bf16(CAPS, 2 * F), bf16(2 * F, CAPS), bf16(CAPS, 128),
        ),
        [SMEM, VMEM, VMEM, ANY, ANY],
        scratch=STAGE_SCRATCH, megabytes=10, flops=3 * DOT_FLOPS, nbytes=8_000_000,
    )(place, near, far, groups[0], groups[1])
    image_1 = image_1.astype(half)
    received_1 = exchange(image_1, second_axis(1))
    caption_near = after(caption_near, image_1)
    image_2, image_3, caption_own, caption_far = call(
        far_stage_kernel,
        (f32(4, F, IMG), f32(4, F, IMG), f32(CAPS // 2, 2 * F), f32(CAPS // 2, 2 * F)),
        [SMEM, VMEM, VMEM, VMEM, ANY, ANY, VMEM],
        scratch=STAGE_SCRATCH, megabytes=10, flops=3 * DOT_FLOPS, nbytes=8_000_000,
    )(place, captions, turned, marks, groups[2], groups[3], caption_near)
    image_2, image_3 = image_2.astype(half), image_3.astype(half)
    caption_far = after(caption_far, (received_1, image_2, image_3))
    crossed = exchange(caption_far, other_core)
    image_received = [
        received_1,
        exchange(image_2, second_axis(2)),
        exchange(image_3, second_axis(3)),
    ]
    group_total = (caption_own + crossed).reshape(4, HALF, 2 * F)
    messages = [group_total[j].astype(half) for j in (2, 1, 3)]
    caption_received = [exchange(m, along_z(j)) for m, j in zip(messages, (2, 1, 3))]
    image_received = after(image_received, messages)
    line = image_own
    for value in image_received:
        line = line + value.astype(jnp.float32)
    both = group_total[0]
    for value in caption_received:
        both = both + value.astype(jnp.float32)
    both = both.astype(jnp.bfloat16)
    mine, theirs = both[:, :F], both[:, F:]
    returned = exchange(theirs, other_half)
    line = after(line, theirs)
    line_received = [exchange(line[j].astype(half), first_axis(j)) for j in (2, 1, 3)]
    total = line[0]
    for value in line_received:
        total = total + value.astype(jnp.float32)
    image_grad = total.astype(jnp.bfloat16).T

    caption_grad = jnp.where(
        xl == 0,
        jnp.concatenate([mine, returned], axis=0),
        jnp.concatenate([returned, mine], axis=0),
    )
    return image_grad, caption_grad


def solution(mesh):
    in_specs = (P("dp", "mp"), P("dp", "mp"), P("dp"), P("dp"), P("dp"))
    out_specs = (P("dp", "mp"), P("dp", "mp"))
    return jax.shard_map(body, mesh=mesh, in_specs=in_specs, out_specs=out_specs, check_vma=False)
```
